512 devices in a mesh: view: 2 (over z_hi), dp: 32 (over x, y), mp: 8 (over z_lo, core).
Axes of the slice: x: 4, y: 8, z: 8 (z_hi: 2, z_lo: 4; z = z_hi * 4 + z_lo), core: 2. Of those that a mesh axis runs over, the one named last changes fastest.
Arguments:
- views: bfloat16 [2, 32768, 768], P('view', ('dp', 'mp')), may hold values from -1 to 1
- prototypes: bfloat16 [768, 4096], P(None, 'mp'), may hold values from -1 to 1
Outputs:
- view_grad: bfloat16 [2, 32768, 768], P('view', ('dp', 'mp'))
- proto_grad: float32 [768, 4096], P(('view', 'dp'), 'mp')
The draws below stay inside these ranges and needn't reach their ends.
All inputs are finite; a program needn't handle non-finite values.
Results may differ from the reference program's by a relative error of at most 0.019.
Values may be sent and summed in bfloat16 or wider, within the bound.
No kernel may reach another device: no remote copies, remote signals or barrier semaphores. Data moves between devices by JAX's collectives and lax.ppermute only.
A program may use at most 64 MiB of HBM per device.

```python
import jax
import jax.numpy as jnp
from jax import lax

D = 768
K = 4096
SWEEPS = 3
B = 32768
N_DP = 32
N_MP = 8


def shared_columns(key):
    return jax.random.truncated_normal(key, -4.0, 4.0, (D, K), jnp.float32) * D ** (-0.5)


def shared_common(key):
    common_key = jax.random.fold_in(key, 11)
    return jax.random.truncated_normal(common_key, -4.0, 4.0, (D,), jnp.float32) * D ** (-0.5)


def draw_prototypes(key, part):
    base = shared_columns(key)
    common = shared_common(key)
    ramp = jnp.arange(K, dtype=jnp.float32) / (K - 1)
    lift = 0.45
    result = base + lift * common[:, None] * ramp[None, :]
    return result.astype(jnp.bfloat16)


def draw_views(key, part):
    base = shared_columns(key)
    common = shared_common(key)
    key = jax.random.fold_in(key, 7)
    keys = jax.random.split(key, 4)
    region_keys = jax.random.split(keys[0], 4)
    region_perm = jax.vmap(lambda one_key: jax.random.permutation(one_key, K))(region_keys)
    picks = jax.random.randint(keys[1], (4, B), 0, K)
    ranked = jnp.min(picks, axis=0).astype(jnp.int32)
    region = jnp.arange(B, dtype=jnp.int32) * 4 // B
    cluster = region_perm[region, ranked]
    centers = jnp.transpose(base[:, cluster])
    shared_part = 0.5
    pull = jnp.full((2, B, 1), 0.45, jnp.float32)
    noise = jax.random.truncated_normal(keys[3], -4.0, 4.0, (2, B, D), jnp.float32) * D ** (-0.5)
    rest = jnp.sqrt(1.0 - pull * pull - shared_part * shared_part)
    result = pull * centers[None] + shared_part * common[None, None, :] + rest * noise
    return result.astype(jnp.bfloat16)


def setup_inputs(seed: int = 0) -> dict:
    splits = jax.random.split(jax.random.key(seed), 3)
    views = draw_views(jax.random.fold_in(splits[2], 71), 0)
    prototypes = draw_prototypes(jax.random.fold_in(splits[2], 71), 0)
    return dict(views=views, prototypes=prototypes)


sink_eps = 0.05
pred_temp = 0.1
grad_scale = 8.0

def column_part(pair):
    block_scores, block_rows = pair
    return lax.optimization_barrier(jnp.sum(jnp.exp(block_scores / sink_eps) * block_rows[:, None], axis=0))

def row_part(pair):
    block_scores, block_cols = pair
    return lax.optimization_barrier(jnp.sum(jnp.exp(block_scores / sink_eps) * block_cols[None, :], axis=1))

def reference(views, prototypes):
    inputs = views.astype(jnp.float32)
    row_norm = jnp.sqrt(lax.optimization_barrier(jnp.sum(inputs * inputs, axis=-1, keepdims=True)) + 1e-06)
    unit_rows = inputs / row_norm
    unit_half = unit_rows.astype(jnp.bfloat16)
    weights = prototypes.astype(jnp.float32)
    proto_norm = jnp.sqrt(lax.optimization_barrier(jnp.sum(weights * weights, axis=0, keepdims=True)) + 1e-06)
    columns = weights / proto_norm
    columns_half = columns.astype(jnp.bfloat16)
    group_rows = views.shape[1] // N_DP
    blocks = unit_half.reshape(2 * N_DP, group_rows, D)
    scores = lax.map(lambda block: jnp.dot(block, columns_half, preferred_element_type=jnp.float32), blocks)
    row_scale = jnp.ones((2 * N_DP, group_rows), jnp.float32)
    col_scale = jnp.ones((2, K), jnp.float32)
    for sweep in range(SWEEPS):
        partial_cols = lax.map(column_part, (scores, row_scale))
        col_scale = 1.0 / lax.optimization_barrier(jnp.sum(partial_cols.reshape(2, N_DP, K), axis=1))
        col_blocks = jnp.repeat(col_scale, N_DP, axis=0)
        row_scale = 1.0 / lax.map(row_part, (scores, col_blocks))
    scores_four = scores.reshape(2, N_DP, group_rows, K)
    rows_three = row_scale.reshape(2, N_DP, group_rows)
    units_four = blocks.reshape(2, N_DP, group_rows, D)
    cols_float = columns_half.astype(jnp.float32).reshape(D, N_MP, K // N_MP)

    def step(column_grad, index):
        block_scores = lax.dynamic_index_in_dim(scores_four, index, 1, keepdims=False)
        block_rows = lax.dynamic_index_in_dim(rows_three, index, 1, keepdims=False)
        block_units = lax.dynamic_index_in_dim(units_four, index, 1, keepdims=False)
        codes = (jnp.exp(block_scores / sink_eps) * col_scale[:, None, :] * block_rows[:, :, None]).astype(jnp.bfloat16)
        expo_pred = jnp.exp(block_scores / pred_temp)
        predicted = expo_pred / lax.optimization_barrier(jnp.sum(expo_pred, axis=-1, keepdims=True))
        grad_half = (grad_scale * (predicted - codes[::-1].astype(jnp.float32)) / pred_temp).astype(jnp.bfloat16)
        grad_float = grad_half.astype(jnp.float32)
        pieces = jnp.einsum('vrmk,dmk->vmrd', grad_float.reshape(2, group_rows, N_MP, K // N_MP), cols_float)
        pieces = lax.optimization_barrier(pieces.astype(jnp.bfloat16)).astype(jnp.float32)
        page_grad = lax.optimization_barrier(jnp.sum(pieces, axis=1))
        unit_float = block_units.astype(jnp.float32)
        column_grad = column_grad + jnp.einsum('vrd,vrk->dk', unit_float, grad_float)
        return (column_grad, page_grad)
    column_grad, pages = lax.scan(step, jnp.zeros((D, K), jnp.float32), jnp.arange(N_DP, dtype=jnp.int32))
    page_grad = jnp.swapaxes(pages, 0, 1).reshape(2, N_DP * group_rows, D)
    inner_rows = lax.optimization_barrier(jnp.sum(unit_rows * page_grad, axis=-1, keepdims=True))
    view_grad = ((page_grad - unit_rows * inner_rows) / row_norm).astype(jnp.bfloat16)
    inner_cols = lax.optimization_barrier(jnp.sum(columns * column_grad, axis=0, keepdims=True))
    proto_grad = (column_grad - columns * inner_cols) / proto_norm
    return (view_grad, proto_grad)
```

```python
import jax
import jax.numpy as jnp
from jax import lax
from jax.sharding import Mesh
from jax.sharding import PartitionSpec as P

SWEEPS = 3

sink_eps = 0.05
pred_temp = 0.1
grad_scale = 8.0

FINE = ("zh", "x", "y", "zl", "core")
DP = ("x", "y")
MP = ("zl", "core")


def swapped(value, axis):
    return lax.ppermute(value, axis, [(0, 1), (1, 0)])


def shared(vector, axes):
    size = lax.axis_size(axes)
    spread = jnp.broadcast_to(vector[None], (size,) + vector.shape)
    return lax.all_to_all(spread, axes, 0, 0, tiled=True)


def on_device(views, prototypes):
    f32, bf16 = jnp.float32, jnp.bfloat16
    inputs = views[0].astype(f32)
    row_norm = jnp.sqrt(jnp.sum(inputs * inputs, axis=-1, keepdims=True) + 1e-06)
    unit_rows = inputs / row_norm
    unit_half = unit_rows.astype(bf16)
    weights = prototypes.astype(f32)
    proto_norm = jnp.sqrt(jnp.sum(weights * weights, axis=0, keepdims=True) + 1e-06)
    columns = weights / proto_norm
    columns_half = columns.astype(bf16)

    rows, width = unit_half.shape
    protos = columns_half.shape[1]
    line = lax.all_gather(unit_half, "zl", axis=0, tiled=False)
    other = swapped(line, "core")
    core = lax.axis_index("core")
    first = jnp.where(core == 0, line, other)
    second = jnp.where(core == 0, other, line)
    grouped = jnp.stack([first, second], axis=1).reshape(-1, width)
    group_rows = grouped.shape[0]

    scores = jnp.dot(grouped, columns_half, preferred_element_type=f32)
    expos = jnp.exp(scores / sink_eps)
    expos, expos_sent = lax.optimization_barrier((expos, expos.astype(bf16)))
    partner_expos = swapped(expos_sent, "zh")
    expo_pred = jnp.exp(scores / pred_temp)

    row_scale = jnp.ones((group_rows,), f32)
    for sweep in range(SWEEPS):
        partial = jnp.sum(expos * row_scale[:, None], axis=0)
        col_scale = 1.0 / jnp.sum(shared(partial, DP), axis=0)
        partial = jnp.sum(expos * col_scale[None, :], axis=1)
        if sweep == 0:
            both = jnp.concatenate([partial, jnp.sum(expo_pred, axis=1)])
            totals = jnp.sum(shared(both, MP), axis=0)
            row_scale = 1.0 / totals[:group_rows]
            pred_total = totals[group_rows:]
        elif sweep < SWEEPS - 1:
            row_scale = 1.0 / jnp.sum(shared(partial, MP), axis=0)
        else:
            partner_cols = swapped(col_scale, "zh")
            mp_size = lax.axis_size(MP)
            pieces = shared(partial, ("zh",) + MP).reshape(2, mp_size, group_rows)
            totals = jnp.sum(pieces, axis=1)
            me = lax.axis_index("zh")
            partner_rows = 1.0 / jnp.where(me == 0, totals[1], totals[0])

    codes = (partner_expos.astype(f32) * partner_cols[None, :] * partner_rows[:, None]).astype(bf16)
    predicted = expo_pred / pred_total[:, None]
    grad_half = (grad_scale * (predicted - codes.astype(f32)) / pred_temp).astype(bf16)

    page_part = lax.dot_general(
        grad_half, columns_half, (((1,), (1,)), ((), ())), preferred_element_type=f32
    ).astype(bf16)
    page_grad = lax.psum_scatter(page_part, MP, scatter_dimension=0, tiled=True).astype(f32)

    column_part = lax.dot_general(
        grouped, grad_half, (((0,), (0,)), ((), ())), preferred_element_type=f32
    )
    shares = lax.axis_size("zh") * lax.axis_size(DP)
    share_rows = width // shares
    column_sent = column_part.astype(bf16)
    inner_part = jnp.sum(columns * column_sent.astype(f32), axis=0)
    inner_high = inner_part.astype(bf16)
    inner_low = (inner_part - inner_high.astype(f32)).astype(bf16)
    inner_rows = jnp.broadcast_to(jnp.stack([inner_high, inner_low])[None], (shares, 2, protos))
    parcels = jnp.concatenate([column_sent.reshape(shares, share_rows, protos), inner_rows], axis=1)
    arrived = lax.all_to_all(parcels, ("zh",) + DP, 0, 0, tiled=True)
    summed = jnp.sum(arrived.astype(f32), axis=0)
    column_grad = summed[:share_rows]
    inner_cols = summed[share_rows] + summed[share_rows + 1]
    start = lax.axis_index(("zh",) + DP) * share_rows
    own_columns = lax.dynamic_slice_in_dim(columns, start, share_rows, 0)
    proto_grad = (column_grad - own_columns * inner_cols[None, :]) / proto_norm

    inner = jnp.sum(unit_rows * page_grad, axis=-1, keepdims=True)
    view_grad = ((page_grad - unit_rows * inner) / row_norm).astype(bf16)[None]
    return (view_grad, proto_grad)


def solution(mesh):
    fine = Mesh(mesh.devices.reshape(2, 4, 8, 4, 2), FINE)
    return jax.shard_map(
        on_device,
        mesh=fine,
        in_specs=(P("zh", DP + MP, None), P(None, MP)),
        out_specs=(P("zh", DP + MP, None), P(("zh",) + DP, MP)),
        check_vma=False,
    )
```

```python
import jax
import jax.numpy as jnp
from jax import lax
from jax.sharding import Mesh
from jax.sharding import PartitionSpec as P

SWEEPS = 3

sink_eps = 0.05
pred_temp = 0.1
grad_scale = 8.0

FINE = ("zh", "x", "y", "zl", "core")
DP = ("x", "y")
MP = ("zl", "core")
LANES = 128


def swapped(value, axis):
    return lax.ppermute(value, axis, [(0, 1), (1, 0)])


def shared(vector, axes):
    size = lax.axis_size(axes)
    tile = vector.reshape(1, -1, LANES)
    spread = jnp.broadcast_to(tile, (size,) + tile.shape[1:])
    return lax.all_to_all(spread, axes, 0, 0, tiled=True)


def over_mp(pieces):
    by_core = jnp.sum(pieces.reshape((lax.axis_size("zl"), 2, 2, -1)), axis=0)
    first = lax.axis_index("core") == 0
    own = jnp.where(first, by_core[0], by_core[1])
    other = jnp.where(first, by_core[1], by_core[0])
    return own + other[::-1]


def high_low(vector, copies):
    high = vector.astype(jnp.bfloat16)
    low = (vector - high.astype(jnp.float32)).astype(jnp.bfloat16)
    return jnp.broadcast_to(jnp.stack([high, low])[None], (copies, 2) + vector.shape)


def on_device(views, prototypes):
    f32, bf16 = jnp.float32, jnp.bfloat16
    inputs = views[0].astype(f32)
    row_norm = jnp.sqrt(jnp.sum(inputs * inputs, axis=-1, keepdims=True) + 1e-06)
    unit_rows = inputs / row_norm
    unit_half = unit_rows.astype(bf16)
    weights = prototypes.astype(f32)
    proto_norm = jnp.sqrt(jnp.sum(weights * weights, axis=0, keepdims=True) + 1e-06)
    columns = weights / proto_norm
    columns_half = columns.astype(bf16)

    width = unit_half.shape[1]
    protos = columns_half.shape[1]
    partner_half = swapped(unit_half, "zh")
    line = lax.all_gather(unit_half, "zl", axis=0, tiled=True)
    grouped = jnp.concatenate([line, swapped(line, "core")], axis=0)
    group_rows = grouped.shape[0]
    half_rows = group_rows // 2

    scores = jnp.dot(grouped, columns_half, preferred_element_type=f32)
    expos = jnp.exp(scores / sink_eps)
    expo_pred = jnp.exp(scores / pred_temp)
    partner_all = lax.all_gather(partner_half, MP, axis=0, tiled=False)
    core = lax.axis_index("core")
    partner_all = partner_all.reshape((-1, 2) + partner_half.shape)

    row_scale = None
    for sweep in range(SWEEPS):
        weighted = expos if row_scale is None else expos * row_scale[:, None]
        partial = jnp.sum(weighted, axis=0)
        pieces = shared(partial, DP)
        col_scale = 1.0 / jnp.sum(pieces, axis=0).reshape(protos)
        partial = jnp.sum(expos * col_scale[None, :], axis=1)
        if sweep == 0:
            both = jnp.stack([partial.reshape(2, half_rows), jnp.sum(expo_pred, axis=1).reshape(2, half_rows)], axis=1)
            totals = over_mp(shared(both, MP)).reshape(2, 2, half_rows)
            row_scale = 1.0 / totals[:, 0].reshape(group_rows)
            pred_total = totals[:, 1].reshape(group_rows)
        elif sweep < SWEEPS - 1:
            row_scale = 1.0 / over_mp(shared(partial, MP)).reshape(group_rows)
        else:
            sent = jnp.concatenate([partial, col_scale])
            pieces = shared(sent, ("zh",) + MP).reshape(2, lax.axis_size(MP), group_rows + protos)
            pieces = lax.dynamic_index_in_dim(pieces, 1 - lax.axis_index("zh"), 0, keepdims=False)
            partner_rows = 1.0 / over_mp(pieces[:, :group_rows]).reshape(group_rows)
            partner_cols = lax.dynamic_index_in_dim(
                pieces[:, group_rows:], lax.axis_index(MP), 0, keepdims=False
            )

    first = lax.dynamic_index_in_dim(partner_all, core, 1, keepdims=False).reshape(half_rows, width)
    second = lax.dynamic_index_in_dim(partner_all, 1 - core, 1, keepdims=False).reshape(half_rows, width)
    partner_group = jnp.concatenate([first, second], axis=0)
    partner_scores = jnp.dot(partner_group, columns_half, preferred_element_type=f32)
    partner_expos = jnp.exp(partner_scores / sink_eps)
    codes = (partner_expos * partner_cols[None, :] * partner_rows[:, None]).astype(bf16)
    predicted = expo_pred / pred_total[:, None]
    grad_half = (grad_scale * (predicted - codes.astype(f32)) / pred_temp).astype(bf16)

    by_columns = (((1,), (1,)), ((), ()))
    other_part = lax.dot_general(
        grad_half[half_rows:], columns_half, by_columns, preferred_element_type=f32
    ).astype(bf16)
    arrived_part = swapped(other_part, "core")
    own_part = lax.dot_general(
        grad_half[:half_rows], columns_half, by_columns, preferred_element_type=f32
    ).astype(bf16)
    page_part = (own_part.astype(f32) + arrived_part.astype(f32)).astype(bf16)
    page_grad = lax.psum_scatter(page_part, "zl", scatter_dimension=0, tiled=True).astype(f32)

    column_part = lax.dot_general(
        grouped, grad_half, (((0,), (0,)), ((), ())), preferred_element_type=f32
    )
    n_zh, n_x, n_y = lax.axis_size("zh"), lax.axis_size("x"), lax.axis_size("y")
    share = width // (n_zh * n_x * n_y)
    column_sent = column_part.astype(bf16)
    inner_part = jnp.sum(columns * column_sent.astype(f32), axis=0)
    parcels = column_sent.reshape(n_zh, n_x, n_y * share, protos).transpose(1, 0, 2, 3)
    parcels = parcels.reshape(n_x, n_zh * n_y * share, protos)
    parcels = jnp.concatenate([parcels, high_low(inner_part, n_x)], axis=1)
    summed = jnp.sum(lax.all_to_all(parcels, "x", 0, 0, tiled=True).astype(f32), axis=0)
    column_sent, inner_part = summed[: n_zh * n_y * share], jnp.sum(summed[n_zh * n_y * share :], axis=0)
    parcels = column_sent.astype(bf16).reshape(n_zh * n_y, share, protos)
    parcels = jnp.concatenate([parcels, high_low(inner_part, n_zh * n_y)], axis=1)
    summed = jnp.sum(lax.all_to_all(parcels, ("zh", "y"), 0, 0, tiled=True).astype(f32), axis=0)
    column_grad = summed[:share]
    inner_cols = jnp.sum(summed[share:], axis=0, keepdims=True)
    start = lax.axis_index(("zh",) + DP) * share
    own_columns = lax.dynamic_slice_in_dim(columns, start, share, 0)
    proto_grad = (column_grad - own_columns * inner_cols) / proto_norm

    inner = jnp.sum(unit_rows * page_grad, axis=-1, keepdims=True)
    view_grad = ((page_grad - unit_rows * inner) / row_norm).astype(bf16)[None]
    return (view_grad, proto_grad)


def solution(mesh):
    fine = Mesh(mesh.devices.reshape(2, 4, 8, 4, 2), FINE)
    return jax.shard_map(
        on_device,
        mesh=fine,
        in_specs=(P("zh", DP + MP, None), P(None, MP)),
        out_specs=(P("zh", DP + MP, None), P(("zh",) + DP, MP)),
        check_vma=False,
    )
```

```python
import jax
import jax.numpy as jnp
from jax import lax
from jax.sharding import Mesh
from jax.sharding import PartitionSpec as P

SWEEPS = 3

sink_eps = 0.05
pred_temp = 0.1
grad_scale = 8.0

FINE = ("zh", "x", "y", "zl", "core")
DP = ("x", "y")
MP = ("zl", "core")
LANES = 128


def swapped(value, axis):
    return lax.ppermute(value, axis, [(0, 1), (1, 0)])


def shared(vector, axes):
    size = lax.axis_size(axes)
    tile = vector.reshape(1, -1, LANES)
    spread = jnp.broadcast_to(tile, (size,) + tile.shape[1:])
    return lax.all_to_all(spread, axes, 0, 0, tiled=True)


def high_low(vector, copies):
    high = vector.astype(jnp.bfloat16)
    low = (vector - high.astype(jnp.float32)).astype(jnp.bfloat16)
    return jnp.broadcast_to(jnp.stack([high, low])[None], (copies, 2) + vector.shape)


def on_device(views, prototypes):
    f32, bf16 = jnp.float32, jnp.bfloat16
    inputs = views[0].astype(f32)
    row_norm = jnp.sqrt(jnp.sum(inputs * inputs, axis=-1, keepdims=True) + 1e-06)
    unit_rows = inputs / row_norm
    unit_half = unit_rows.astype(bf16)
    weights = prototypes.astype(f32)
    proto_norm = jnp.sqrt(jnp.sum(weights * weights, axis=0, keepdims=True) + 1e-06)
    columns = weights / proto_norm
    columns_half = columns.astype(bf16)

    width = unit_half.shape[1]
    protos = columns_half.shape[1]
    partner_half = swapped(unit_half, "zh")
    core = lax.axis_index("core")
    zh = lax.axis_index("zh")

    def interleaved(own, other):
        first, second = jnp.where(core == 0, own, other), jnp.where(core == 0, other, own)
        return jnp.stack([first, second], axis=1).reshape(-1, width)

    line = lax.all_gather(unit_half, "zl", axis=0, tiled=False)
    grouped = interleaved(line, swapped(line, "core"))
    group_rows = grouped.shape[0]

    to_scores = (((0,), (1,)), ((), ()))
    scores = lax.dot_general(columns_half, grouped, to_scores, preferred_element_type=f32)
    expos = jnp.exp(scores / sink_eps)
    expo_pred = jnp.exp(scores / pred_temp)
    partner_group = lax.all_gather(partner_half, MP, axis=0, tiled=True)

    row_scale = None
    for sweep in range(SWEEPS):
        weighted = expos if row_scale is None else expos * row_scale[None, :]
        pieces = shared(jnp.sum(weighted, axis=1), DP)
        col_scale = 1.0 / jnp.sum(pieces, axis=0).reshape(protos)
        partial = jnp.sum(expos * col_scale[:, None], axis=0)
        if sweep == 0:
            both = jnp.concatenate([partial, jnp.sum(expo_pred, axis=0)])
            totals = jnp.sum(shared(both, MP), axis=0).reshape(2, group_rows)
            row_scale = 1.0 / totals[0]
            pred_scale = 1.0 / totals[1]
        elif sweep < SWEEPS - 1:
            row_scale = 1.0 / jnp.sum(shared(partial, MP), axis=0).reshape(group_rows)
        else:
            sent = jnp.concatenate([partial, col_scale, pred_scale])
            pieces = shared(sent, ("zh",) + MP).reshape(2, lax.axis_size(MP), -1)
            row_scales = 1.0 / jnp.sum(pieces[:, :, :group_rows], axis=1)
            row_scale = jnp.where(zh == 0, row_scales[0], row_scales[1])
            partner_rows = jnp.where(zh == 0, row_scales[1], row_scales[0])
            pieces = lax.dynamic_index_in_dim(pieces, 1 - zh, 0, keepdims=False)
            pieces = lax.dynamic_index_in_dim(pieces, lax.axis_index(MP), 0, keepdims=False)
            partner_cols = pieces[group_rows : group_rows + protos]
            partner_pred = pieces[group_rows + protos :]

    def grads(own_scores, own_pred, code_scores, code_cols, code_rows):
        predicted = jnp.exp(own_scores / pred_temp) * own_pred[None, :]
        codes = (jnp.exp(code_scores / sink_eps) * code_cols[:, None] * code_rows[None, :]).astype(bf16)
        return (grad_scale * (predicted - codes.astype(f32)) / pred_temp).astype(bf16)

    def mine(array):
        return lax.dynamic_slice_in_dim(array, zh * (protos // 2), protos // 2, 0)

    partner_scores = lax.dot_general(columns_half, partner_group, to_scores, preferred_element_type=f32)
    grad_half = grads(scores, pred_scale, partner_scores, partner_cols, partner_rows)
    partner_grad = grads(mine(partner_scores), partner_pred, mine(scores), mine(col_scale), row_scale)

    page_part = lax.dot_general(grad_half, columns_half, to_scores, preferred_element_type=f32).astype(bf16)
    page_grad = lax.psum_scatter(page_part, MP, scatter_dimension=0, tiled=True).astype(f32)

    by_pages = (((0,), (1,)), ((), ()))
    column_part = lax.dot_general(
        grouped, mine(grad_half), by_pages, preferred_element_type=f32
    ) + lax.dot_general(partner_group, partner_grad, by_pages, preferred_element_type=f32)
    n_zh, n_x, n_y = lax.axis_size("zh"), lax.axis_size("x"), lax.axis_size("y")
    share = width // (n_zh * n_x * n_y)
    half = protos // 2
    column_sent = column_part.astype(bf16)
    inner_part = jnp.sum(lax.dynamic_slice_in_dim(columns, zh * half, half, 1) * column_sent.astype(f32), axis=0)
    parcels = column_sent.reshape(n_zh, n_x, n_y * share, half).transpose(1, 0, 2, 3)
    parcels = parcels.reshape(n_x, n_zh * n_y * share, half)
    parcels = jnp.concatenate([parcels, high_low(inner_part, n_x)], axis=1)
    summed = jnp.sum(lax.all_to_all(parcels, "x", 0, 0, tiled=True).astype(f32), axis=0)
    column_sent, inner_part = summed[: n_zh * n_y * share], jnp.sum(summed[n_zh * n_y * share :], axis=0)
    parcels = column_sent.astype(bf16).reshape(n_zh * n_y, share, half)
    parcels = jnp.concatenate([parcels, high_low(inner_part, n_zh * n_y)], axis=1)
    arrived = lax.all_to_all(parcels, ("zh", "y"), 0, 0, tiled=True).astype(f32)
    summed = jnp.sum(arrived.reshape(n_zh, n_y, share + 2, half), axis=1)
    summed = jnp.concatenate([summed[0], summed[1]], axis=1)
    column_grad = summed[:share]
    inner_cols = jnp.sum(summed[share:], axis=0, keepdims=True)
    start = lax.axis_index(("zh",) + DP) * share
    own_columns = lax.dynamic_slice_in_dim(columns, start, share, 0)
    proto_grad = (column_grad - own_columns * inner_cols) / proto_norm

    inner = jnp.sum(unit_rows * page_grad, axis=-1, keepdims=True)
    view_grad = ((page_grad - unit_rows * inner) / row_norm).astype(bf16)[None]
    return (view_grad, proto_grad)


def solution(mesh):
    fine = Mesh(mesh.devices.reshape(2, 4, 8, 4, 2), FINE)
    return jax.shard_map(
        on_device,
        mesh=fine,
        in_specs=(P("zh", DP + MP, None), P(None, MP)),
        out_specs=(P("zh", DP + MP, None), P(("zh",) + DP, MP)),
        check_vma=False,
    )
```

```python
import jax
import jax.numpy as jnp
from jax import lax
from jax.experimental import pallas as pl
from jax.experimental.pallas import tpu as pltpu
from jax.sharding import Mesh
from jax.sharding import PartitionSpec as P

SWEEPS = 3

sink_eps = 0.05
pred_temp = 0.1
grad_scale = 8.0

FINE = ("zh", "x", "y", "zl", "core")
DP = ("x", "y")
MP = ("zl", "core")
LANES = 128


def swapped(value, axis):
    return lax.ppermute(value, axis, [(0, 1), (1, 0)])


def shared(vector, axes):
    size = lax.axis_size(axes)
    tile = vector.reshape(1, -1, LANES)
    spread = jnp.broadcast_to(tile, (size,) + tile.shape[1:])
    return lax.all_to_all(spread, axes, 0, 0, tiled=True)


def high_low(vector, copies):
    high = vector.astype(jnp.bfloat16)
    low = (vector - high.astype(jnp.float32)).astype(jnp.bfloat16)
    return jnp.broadcast_to(jnp.stack([high, low])[None], (copies, 2) + vector.shape)


def view_grad_kernel(views, page_grad, out):
    f32 = jnp.float32
    inputs = views[0].astype(f32)
    row_norm = jnp.sqrt(jnp.sum(inputs * inputs, axis=-1, keepdims=True) + 1e-06)
    unit_rows = inputs / row_norm
    page = page_grad[...].astype(f32)
    inner = jnp.sum(unit_rows * page, axis=-1, keepdims=True)
    out[0] = ((page - unit_rows * inner) / row_norm).astype(out.dtype)


def unit_kernel(views, out):
    inputs = views[0].astype(jnp.float32)
    row_norm = jnp.sqrt(jnp.sum(inputs * inputs, axis=-1, keepdims=True) + 1e-06)
    out[...] = (inputs / row_norm).astype(out.dtype)


def on_device(views, prototypes):
    f32, bf16 = jnp.float32, jnp.bfloat16
    unit_half = pl.pallas_call(
        unit_kernel,
        out_shape=jax.ShapeDtypeStruct(views.shape[1:], bf16),
        compiler_params=pltpu.CompilerParams(vmem_limit_bytes=4 * 2**20),
        name="unit_rows",
    )(views)
    weights = prototypes.astype(f32)
    proto_norm = jnp.sqrt(jnp.sum(weights * weights, axis=0, keepdims=True) + 1e-06)
    columns = weights / proto_norm
    columns_half = columns.astype(bf16)

    width = unit_half.shape[1]
    protos = columns_half.shape[1]
    partner_half = swapped(unit_half, "zh")
    core = lax.axis_index("core")
    zh = lax.axis_index("zh")

    def interleaved(own, other):
        blocks = (-1, 1) + unit_half.shape
        first, second = jnp.where(core == 0, own, other), jnp.where(core == 0, other, own)
        return jnp.concatenate([first.reshape(blocks), second.reshape(blocks)], axis=1).reshape(-1, width)

    line = lax.all_gather(unit_half, "zl", axis=0, tiled=True)
    grouped = interleaved(line, swapped(line, "core"))
    group_rows = grouped.shape[0]

    to_scores = (((0,), (1,)), ((), ()))
    scores = lax.dot_general(columns_half, grouped, to_scores, preferred_element_type=f32)
    expos = jnp.exp(scores / sink_eps)
    expo_pred = jnp.exp(scores / pred_temp)
    partner_group = lax.all_gather(partner_half, MP, axis=0, tiled=True)

    row_scale = None
    for sweep in range(SWEEPS):
        weighted = expos if row_scale is None else expos * row_scale[None, :]
        pieces = shared(jnp.sum(weighted, axis=1), DP)
        col_scale = 1.0 / jnp.sum(pieces, axis=0).reshape(protos)
        partial = jnp.sum(expos * col_scale[:, None], axis=0)
        if sweep == 0:
            both = jnp.concatenate([partial, jnp.sum(expo_pred, axis=0)])
            totals = jnp.sum(shared(both, MP), axis=0).reshape(2, group_rows)
            row_scale = 1.0 / totals[0]
            pred_scale = 1.0 / totals[1]
        elif sweep < SWEEPS - 1:
            row_scale = 1.0 / jnp.sum(shared(partial, MP), axis=0).reshape(group_rows)
        else:
            sent = jnp.concatenate([partial, col_scale, pred_scale])
            pieces = shared(sent.astype(bf16), ("zh",) + MP).astype(f32).reshape(2, lax.axis_size(MP), -1)
            row_scales = 1.0 / jnp.sum(pieces[:, :, :group_rows], axis=1)
            row_scale = jnp.where(zh == 0, row_scales[0], row_scales[1])
            partner_rows = jnp.where(zh == 0, row_scales[1], row_scales[0])
            pieces = lax.dynamic_index_in_dim(pieces, 1 - zh, 0, keepdims=False)
            pieces = lax.dynamic_index_in_dim(pieces, lax.axis_index(MP), 0, keepdims=False)
            partner_cols = pieces[group_rows : group_rows + protos]
            partner_pred = pieces[group_rows + protos :]

    def grads(own_scores, own_pred, code_scores, code_cols, code_rows):
        predicted = jnp.exp(own_scores / pred_temp) * own_pred[None, :]
        codes = (jnp.exp(code_scores / sink_eps) * code_cols[:, None] * code_rows[None, :]).astype(bf16)
        return (grad_scale * (predicted - codes.astype(f32)) / pred_temp).astype(bf16)

    def mine(array):
        return lax.dynamic_slice_in_dim(array, zh * (protos // 2), protos // 2, 0)

    my_columns = lax.dynamic_slice_in_dim(columns_half, zh * (protos // 2), protos // 2, 1)

    partner_scores = lax.dot_general(columns_half, partner_group, to_scores, preferred_element_type=f32)
    grad_half = grads(scores, pred_scale, partner_scores, partner_cols, partner_rows)
    page_part = lax.dot_general(grad_half, columns_half, to_scores, preferred_element_type=f32).astype(bf16)
    page_grad = lax.psum_scatter(page_part, MP, scatter_dimension=0, tiled=True)

    my_scores = mine(scores)
    my_partner = lax.dot_general(my_columns, partner_group, to_scores, preferred_element_type=f32)
    my_grad = grads(my_scores, pred_scale, my_partner, mine(partner_cols), partner_rows)
    partner_grad = grads(my_partner, partner_pred, my_scores, mine(col_scale), row_scale)
    by_pages = (((0,), (1,)), ((), ()))
    column_part = lax.dot_general(
        grouped, my_grad, by_pages, preferred_element_type=f32
    ) + lax.dot_general(partner_group, partner_grad, by_pages, preferred_element_type=f32)

    n_zh, n_x, n_y = lax.axis_size("zh"), lax.axis_size("x"), lax.axis_size("y")
    share = width // (n_zh * n_x * n_y)
    half = protos // 2
    column_sent = column_part.astype(bf16)
    inner_part = jnp.sum(lax.dynamic_slice_in_dim(columns, zh * half, half, 1) * column_sent.astype(f32), axis=0)
    parcels = column_sent.reshape(n_zh, n_x, n_y * share, half).transpose(1, 0, 2, 3)
    parcels = parcels.reshape(n_x, n_zh * n_y * share, half)
    parcels = jnp.concatenate([parcels, high_low(inner_part, n_x)], axis=1)
    summed = jnp.sum(lax.all_to_all(parcels, "x", 0, 0, tiled=True).astype(f32), axis=0)
    column_sent, inner_part = summed[: n_zh * n_y * share], jnp.sum(summed[n_zh * n_y * share :], axis=0)
    parcels = column_sent.astype(bf16).reshape(n_zh * n_y, share, half)
    parcels = jnp.concatenate([parcels, high_low(inner_part, n_zh * n_y)], axis=1)
    arrived = lax.all_to_all(parcels, ("zh", "y"), 0, 0, tiled=True).astype(f32)
    summed = jnp.sum(arrived.reshape(n_zh, n_y, share + 2, half), axis=1)
    summed = jnp.concatenate([summed[0], summed[1]], axis=1)
    column_grad = summed[:share]
    inner_cols = jnp.sum(summed[share:], axis=0, keepdims=True)
    start = lax.axis_index(("zh",) + DP) * share
    own_columns = lax.dynamic_slice_in_dim(columns, start, share, 0)
    proto_grad = (column_grad - own_columns * inner_cols) / proto_norm

    view_grad = pl.pallas_call(
        view_grad_kernel,
        out_shape=jax.ShapeDtypeStruct(views.shape, views.dtype),
        compiler_params=pltpu.CompilerParams(vmem_limit_bytes=4 * 2**20),
        name="view_grad",
    )(views, page_grad)
    return (view_grad, proto_grad)


def solution(mesh):
    fine = Mesh(mesh.devices.reshape(2, 4, 8, 4, 2), FINE)
    return jax.shard_map(
        on_device,
        mesh=fine,
        in_specs=(P("zh", DP + MP, None), P(None, MP)),
        out_specs=(P("zh", DP + MP, None), P(("zh",) + DP, MP)),
        check_vma=False,
    )
```

```python
import jax
import jax.numpy as jnp
from jax import lax
from jax.experimental import pallas as pl
from jax.experimental.pallas import tpu as pltpu
from jax.sharding import Mesh
from jax.sharding import PartitionSpec as P

SWEEPS = 3

sink_eps = 0.05
pred_temp = 0.1
grad_scale = 8.0

FINE = ("zh", "x", "y", "zl", "core")
DP = ("x", "y")
MP = ("zl", "core")
LANES = 128


def swapped(value, axis):
    return lax.ppermute(value, axis, [(0, 1), (1, 0)])


def shared(vector, axes, kind=jnp.bfloat16):
    size = lax.axis_size(axes)
    tile = vector.astype(kind).reshape(1, -1, LANES)
    spread = jnp.broadcast_to(tile, (size,) + tile.shape[1:])
    return lax.all_to_all(spread, axes, 0, 0, tiled=True).astype(jnp.float32)


def view_grad_kernel(views, page_grad, out):
    f32 = jnp.float32
    inputs = views[0].astype(f32)
    row_norm = jnp.sqrt(jnp.sum(inputs * inputs, axis=-1, keepdims=True) + 1e-06)
    unit_rows = inputs / row_norm
    page = page_grad[...].astype(f32)
    inner = jnp.sum(unit_rows * page, axis=-1, keepdims=True)
    out[0] = ((page - unit_rows * inner) / row_norm).astype(out.dtype)


def unit_kernel(views, out):
    inputs = views[0].astype(jnp.float32)
    row_norm = jnp.sqrt(jnp.sum(inputs * inputs, axis=-1, keepdims=True) + 1e-06)
    out[...] = (inputs / row_norm).astype(out.dtype)


def on_device(views, prototypes):
    f32, bf16 = jnp.float32, jnp.bfloat16
    unit_half = pl.pallas_call(
        unit_kernel,
        out_shape=jax.ShapeDtypeStruct(views.shape[1:], bf16),
        compiler_params=pltpu.CompilerParams(vmem_limit_bytes=4 * 2**20),
        name="unit_rows",
    )(views)
    weights = prototypes.astype(f32)
    proto_norm = jnp.sqrt(jnp.sum(weights * weights, axis=0, keepdims=True) + 1e-06)
    columns = weights / proto_norm
    columns_half = columns.astype(bf16)

    width = unit_half.shape[1]
    protos = columns_half.shape[1]
    partner_half = swapped(unit_half, "zh")
    core = lax.axis_index("core")
    zh = lax.axis_index("zh")

    line = lax.all_gather(unit_half, "zl", axis=0, tiled=False)
    other = swapped(line, "core")
    by_chip = jnp.zeros(line.shape[:1] + (2,) + line.shape[1:], bf16)
    by_chip = lax.dynamic_update_index_in_dim(by_chip, line, core, 1)
    by_chip = lax.dynamic_update_index_in_dim(by_chip, other, 1 - core, 1)
    grouped = by_chip.reshape(-1, width)
    group_rows = grouped.shape[0]
    to_scores = (((0,), (1,)), ((), ()))
    scores = lax.dot_general(columns_half, grouped, to_scores, preferred_element_type=f32)
    expos = jnp.exp(scores / sink_eps)
    expo_pred = jnp.exp(scores / pred_temp)
    partner_group = lax.all_gather(partner_half, MP, axis=0, tiled=True)

    row_scale = None
    for sweep in range(SWEEPS):
        weighted = expos if row_scale is None else expos * row_scale[None, :]
        pieces = shared(jnp.sum(weighted, axis=1), DP, f32)
        col_scale = 1.0 / jnp.sum(pieces, axis=0).reshape(protos)
        partial = jnp.sum(expos * col_scale[:, None], axis=0)
        if sweep == 0:
            both = jnp.concatenate([partial, jnp.sum(expo_pred, axis=0)])
            totals = jnp.sum(shared(both, MP), axis=0).reshape(2, group_rows)
            row_scale = 1.0 / totals[0]
            pred_scale = 1.0 / totals[1]
        elif sweep < SWEEPS - 1:
            row_scale = 1.0 / jnp.sum(shared(partial, MP), axis=0).reshape(group_rows)
        else:
            sent = jnp.concatenate([partial, col_scale, pred_scale])
            pieces = shared(sent, ("zh",) + MP).reshape(2, lax.axis_size(MP), -1)
            row_scales = 1.0 / jnp.sum(pieces[:, :, :group_rows], axis=1)
            row_scale = jnp.where(zh == 0, row_scales[0], row_scales[1])
            partner_rows = jnp.where(zh == 0, row_scales[1], row_scales[0])
            pieces = lax.dynamic_index_in_dim(pieces, 1 - zh, 0, keepdims=False)
            pieces = lax.dynamic_index_in_dim(pieces, lax.axis_index(MP), 0, keepdims=False)
            partner_cols = pieces[group_rows : group_rows + protos]
            partner_pred = pieces[group_rows + protos :]

    def grads(own_scores, own_pred, code_scores, code_cols, code_rows):
        predicted = jnp.exp(own_scores / pred_temp) * own_pred[None, :]
        codes = (jnp.exp(code_scores / sink_eps) * code_cols[:, None] * code_rows[None, :]).astype(bf16)
        return (grad_scale * (predicted - codes.astype(f32)) / pred_temp).astype(bf16)

    def mine(array):
        return lax.dynamic_slice_in_dim(array, zh * (protos // 2), protos // 2, 0)

    my_columns = lax.dynamic_slice_in_dim(columns_half, zh * (protos // 2), protos // 2, 1)

    partner_scores = lax.dot_general(columns_half, partner_group, to_scores, preferred_element_type=f32)
    grad_half = grads(scores, pred_scale, partner_scores, partner_cols, partner_rows)
    page_part = lax.dot_general(grad_half, columns_half, to_scores, preferred_element_type=f32).astype(bf16)
    page_grad = lax.psum_scatter(page_part, MP, scatter_dimension=0, tiled=True)

    my_scores = mine(scores)
    my_partner = lax.dot_general(my_columns, partner_group, to_scores, preferred_element_type=f32)
    my_grad = grads(my_scores, pred_scale, my_partner, mine(partner_cols), partner_rows)
    partner_grad = grads(my_partner, partner_pred, my_scores, mine(col_scale), row_scale)
    by_pages = (((0,), (1,)), ((), ()))
    column_part = lax.dot_general(
        grouped, my_grad, by_pages, preferred_element_type=f32
    ) + lax.dot_general(partner_group, partner_grad, by_pages, preferred_element_type=f32)

    n_zh, n_x, n_y = lax.axis_size("zh"), lax.axis_size("x"), lax.axis_size("y")
    share = width // (n_zh * n_x * n_y)
    half = protos // 2
    exact = lax.dynamic_slice_in_dim(columns, zh * half, half, 1)
    inner = jnp.sum(exact * column_part, axis=0, keepdims=True)
    column_sent = (column_part - exact * inner).astype(bf16)
    parcels = column_sent.reshape(n_zh, n_x, n_y * share, half).transpose(1, 0, 2, 3)
    parcels = parcels.reshape(n_x, n_zh * n_y * share, half)
    summed = jnp.sum(lax.all_to_all(parcels, "x", 0, 0, tiled=True).astype(f32), axis=0)
    parcels = summed.astype(bf16).reshape(n_zh * n_y, share, half)
    arrived = lax.all_to_all(parcels, ("zh", "y"), 0, 0, tiled=True).astype(f32)
    summed = jnp.sum(arrived.reshape(n_zh, n_y, share, half), axis=1)
    proto_grad = jnp.concatenate([summed[0], summed[1]], axis=1) / proto_norm

    view_grad = pl.pallas_call(
        view_grad_kernel,
        out_shape=jax.ShapeDtypeStruct(views.shape, views.dtype),
        compiler_params=pltpu.CompilerParams(vmem_limit_bytes=4 * 2**20),
        name="view_grad",
    )(views, page_grad)
    return (view_grad, proto_grad)


def solution(mesh):
    fine = Mesh(mesh.devices.reshape(2, 4, 8, 4, 2), FINE)
    return jax.shard_map(
        on_device,
        mesh=fine,
        in_specs=(P("zh", DP + MP, None), P(None, MP)),
        out_specs=(P("zh", DP + MP, None), P(("zh",) + DP, MP)),
        check_vma=False,
    )
```
